32 devices in a mesh: ctx: 8 (over y, x, core), head: 4 (over z).
Axes of the slice: x: 2, y: 2, z: 4, core: 2. Of those that a mesh axis runs over, the one named last changes fastest.
Arguments:
- queries: bfloat16 [2, 4096, 2560], P(None, ('ctx', 'head')), may hold values from -6 to 6
- keys: bfloat16 [2, 4096, 2560], P(None, ('ctx', 'head')), may hold values from -6 to 6
- values: bfloat16 [2, 4096, 2560], P(None, ('ctx', 'head')), may hold values from -6 to 6
- rates: bfloat16 [2, 4096, 4], P(None, ('ctx', 'head')), may hold values from 0.00018501282 to 0.0018463135
- gate_fast: float32 [4, 640, 640], P('head'), may hold values from -0.25 to 0.25
- up_fast: float32 [4, 640, 640], P('head'), may hold values from -0.25 to 0.25
- down_fast: float32 [4, 640, 640], P('head'), may hold values from -0.25 to 0.25
- out_gain: float32 [2560], P('head'), may hold values from 0.5 to 1.5
- out_proj: bfloat16 [2560, 2560], P('head'), may hold values from -0.125 to 0.125
Outputs:
- mixed: bfloat16 [2, 4096, 2560], P(None, ('ctx', 'head'))
The draws below stay inside these ranges and needn't reach their ends.
All inputs are finite; a program needn't handle non-finite values.
Results may differ from the reference program's by a relative error of at most 0.014.
Values may be sent and summed in bfloat16 or wider, within the bound.
A program may use at most 128 MiB of HBM per device.

```python
import math
import jax
import jax.numpy as jnp
from jax import lax

HD = 640
BLOCKS = 2
HEADS = 4
D = 2560
BLOCK = 4096


def steps_of(rng, extent, split, low, largest):
    loudness = 1.0
    for position, parts in split:
        heights = jax.random.uniform(jax.random.fold_in(jax.random.fold_in(rng, 6), position), (parts,), jnp.float32, low / len(split), largest / len(split))
        loudness = loudness * jnp.repeat(jnp.exp(heights), extent[position] // parts).reshape((-1,) + (1,) * (len(extent) - 1 - position))
    return loudness


def normal_values(key, shape, deviation, limit, cuts=(), held_as=jnp.bfloat16):
    entries = jax.random.normal(key, shape, jnp.float32) * deviation
    if len(cuts) > 0:
        entries = steps_of(key, shape, cuts, -0.22, 0.18) * entries
    return jnp.clip(entries, min=-limit, max=limit).astype(held_as)


def setup_inputs(seed: int = 0) -> dict:
    key_of = jax.random.split(jax.random.key(seed), 10)
    return {
        "queries": normal_values(key_of[0], (BLOCKS, BLOCK, D), 1.0, 6.0, ((1, 32),)),
        "keys": normal_values(key_of[1], (BLOCKS, BLOCK, D), 1.0, 6.0, ((1, 32),)),
        "values": normal_values(key_of[2], (BLOCKS, BLOCK, D), 1.0, 6.0, ((1, 32),)),
        "rates": jnp.clip(jnp.exp(math.log(0.0018463135) - 2.3005211 * jax.random.uniform(key_of[3], (BLOCKS, BLOCK, HEADS), jnp.float32) ** steps_of(key_of[3], (BLOCKS, BLOCK, HEADS), ((1, 32),), -0.2, 0.2)), 0.00018501282, 0.0018463135).astype(jnp.bfloat16),
        "gate_fast": normal_values(key_of[4], (HEADS, HD, HD), HD ** -0.5, 0.25, ((0, 4),), jnp.float32),
        "up_fast": normal_values(key_of[5], (HEADS, HD, HD), HD ** -0.5, 0.25, ((0, 4),), jnp.float32),
        "down_fast": normal_values(key_of[6], (HEADS, HD, HD), HD ** -0.5, 0.25, ((0, 4),), jnp.float32),
        "out_gain": jnp.clip(1.0 + 0.1 * jax.random.normal(key_of[7], (D,), jnp.float32), 0.5, 1.5),
        "out_proj": normal_values(key_of[8], (D, D), D ** -0.5, 0.125, ((0, 4),)),
    }


highest = lax.Precision.HIGHEST

def matmul(left, right):
    return jnp.dot(left, right, precision=highest, preferred_element_type=jnp.float32)

def contract_rows(left, right):
    return lax.dot_general(left, right, (((0,), (0,)), ((), ())), precision=highest, preferred_element_type=jnp.float32)

def contract_cols(left, right):
    return lax.dot_general(left, right, (((1,), (1,)), ((), ())), precision=highest, preferred_element_type=jnp.float32)

def fast_grads(key_rows, value_rows, rate_rows, w_gate, w_up, w_down):
    pre_gate = matmul(key_rows, w_gate)
    pre_up = matmul(key_rows, w_up)
    sigma = jax.nn.sigmoid(pre_gate)
    silu_gate = pre_gate * sigma
    hidden = silu_gate * pre_up
    target = value_rows * rate_rows[:, None]
    grad_down = contract_rows(hidden, target)
    back = contract_cols(target, w_down)
    grad_gate = contract_rows(key_rows, back * pre_up * sigma * (1.0 + pre_gate * (1.0 - sigma)))
    grad_up = contract_rows(key_rows, back * silu_gate)
    return (grad_gate, grad_up, grad_down)

def renorm(matrix, target_norm):
    return matrix * (target_norm * lax.rsqrt(lax.optimization_barrier(jnp.sum(matrix * matrix, axis=-2)) + 1e-06))[..., None, :]

def fast_apply(query_rows, w_gate, w_up, w_down):
    pre_gate = matmul(query_rows, w_gate)
    hidden = pre_gate * jax.nn.sigmoid(pre_gate) * matmul(query_rows, w_up)
    return matmul(hidden, w_down)

def head_norm(out_rows, gain_rows):
    return out_rows * lax.rsqrt(lax.optimization_barrier(jnp.mean(out_rows * out_rows, axis=-1, keepdims=True)) + 1e-05) * gain_rows

def reference(queries, keys, values, rates, gate_fast, up_fast, down_fast, out_gain, out_proj):
    normed_all = [[] for block_index in range(BLOCKS)]
    for head_index in range(HEADS):
        col_start = head_index * HD
        col_stop = col_start + HD
        weights = (gate_fast[head_index], up_fast[head_index], down_fast[head_index])
        norms = tuple((jnp.sqrt(lax.optimization_barrier(jnp.sum(matrix * matrix, axis=0))) for matrix in weights))
        for block_index in range(BLOCKS):
            key_rows = keys[block_index, :, col_start:col_stop].astype(jnp.float32)
            value_rows = values[block_index, :, col_start:col_stop].astype(jnp.float32)
            query_rows = queries[block_index, :, col_start:col_stop].astype(jnp.float32)
            rate_rows = rates[block_index, :, head_index].astype(jnp.float32)
            grads = fast_grads(key_rows, value_rows, rate_rows, weights[0], weights[1], weights[2])
            weights = tuple((renorm(matrix + grad, norm) for matrix, grad, norm in zip(weights, grads, norms)))
            out_rows = fast_apply(query_rows, weights[0], weights[1], weights[2])
            normed_all[block_index].append(head_norm(out_rows, out_gain[col_start:col_stop]).astype(jnp.bfloat16))
    mixed = []
    for block_index in range(BLOCKS):
        normed = jnp.concatenate(normed_all[block_index], axis=1)
        mixed.append(jnp.dot(normed, out_proj, preferred_element_type=jnp.float32).astype(jnp.bfloat16))
    return jnp.stack(mixed, 0)
```

```python
import jax
import jax.numpy as jnp
from jax import lax
from jax.sharding import PartitionSpec as P

bf16 = jnp.bfloat16
f32 = jnp.float32


def dot(left, right, dims):
    return lax.dot_general(
        left.astype(f32), right.astype(f32), (dims, ((), ())), precision=lax.Precision.HIGH, preferred_element_type=f32
    )


def fast_grads(key, target, gate, up, down):
    pre_gate = dot(key, gate, ((1,), (0,)))
    pre_up = dot(key, up, ((1,), (0,)))
    sigma = jax.nn.sigmoid(pre_gate)
    silu_gate = pre_gate * sigma
    hidden = silu_gate * pre_up
    grad_down = dot(hidden, target, ((0,), (0,)))
    back = dot(target, down, ((1,), (1,)))
    d_gate = back * pre_up * sigma * (1.0 + pre_gate * (1.0 - sigma))
    grad_gate = dot(key, d_gate, ((0,), (0,)))
    grad_up = dot(key, back * silu_gate, ((0,), (0,)))
    return grad_gate, grad_up, grad_down


def renorm(matrix, norm):
    return matrix * (norm * lax.rsqrt(jnp.sum(matrix * matrix, axis=0) + 1e-06))[None, :]


def fast_apply(query, gate, up, down, gain):
    pre_gate = dot(query, gate, ((1,), (0,)))
    hidden = pre_gate * jax.nn.sigmoid(pre_gate) * dot(query, up, ((1,), (0,)))
    out = dot(hidden, down, ((1,), (0,)))
    scale = lax.rsqrt(jnp.mean(out * out, axis=-1, keepdims=True) + 1e-05)
    return (out * scale * gain[None, :]).astype(bf16)


def gather_proj(out_proj):
    cols = out_proj.shape[1] // lax.axis_size("ctx")
    piece = lax.dynamic_slice_in_dim(out_proj, lax.axis_index("ctx") * cols, cols, 1)
    piece = lax.all_gather(piece, "head", axis=0, tiled=True)
    return lax.all_gather(piece, "ctx", axis=1, tiled=True)


def per_device(queries, keys, values, rates, gate_fast, up_fast, down_fast, out_gain, out_proj):
    blocks, share, _ = queries.shape
    width = gate_fast.shape[1]
    heads = lax.axis_size("head")
    targets = (
        values.astype(f32).reshape(blocks, share, heads, width) * rates.astype(f32)[..., None]
    ).astype(bf16).reshape(values.shape)

    def to_head(x):
        return lax.all_to_all(x, "head", split_axis=1, concat_axis=0, tiled=True)

    weights = [gate_fast[0], up_fast[0], down_fast[0]]
    norms = [jnp.sqrt(jnp.sum(m * m, axis=0)) for m in weights]
    proj = gather_proj(out_proj)
    outs = []
    for b in range(blocks):
        grads = fast_grads(to_head(keys[b]), to_head(targets[b]), *weights)
        totals = lax.psum(grads, "ctx")
        weights = [renorm(m + t, n) for m, t, n in zip(weights, totals, norms)]
        normed = fast_apply(to_head(queries[b]), *weights, out_gain)
        outs.append(lax.all_to_all(normed, "head", split_axis=0, concat_axis=1, tiled=True))
    normed = jnp.stack(outs, 0)
    return jnp.einsum("btf,fd->btd", normed, proj, preferred_element_type=f32).astype(bf16)


def solution(mesh):
    tokens = P(None, ("ctx", "head"), None)
    matrix = P("head", None, None)
    return jax.shard_map(
        per_device,
        mesh=mesh,
        in_specs=(tokens,) * 4 + (matrix,) * 3 + (P("head"), P("head", None)),
        out_specs=tokens,
        check_vma=False,
    )
```

```python
import functools

import jax
import jax.numpy as jnp
from jax import lax
from jax.experimental import pallas as pl
from jax.experimental.pallas import tpu as pltpu
from jax.sharding import PartitionSpec as P

bf16 = jnp.bfloat16
f32 = jnp.float32
MESH = pl.DeviceIdType.MESH
NN = (((1,), (0,)), ((), ()))
NT = (((1,), (1,)), ((), ()))
TN = (((0,), (0,)), ((), ()))
TILE = 128


def dot(left, right, dims):
    return lax.dot_general(left, right, dims, preferred_element_type=f32)


def dot_split(left, right, dims):
    high = left.astype(bf16)
    low = (left - high.astype(f32)).astype(bf16)
    return dot(high, right, dims) + dot(low, right, dims)


def kernel(
    n_ctx, n_head, rows,
    q_ref, k_ref, v_ref, r_ref, g_ref, u_ref, d_ref, gain_ref,
    o_ref,
    tgt, kx, tx, qx, wb, wt, mst, gb, rb1, sb, rb2, dgu, hid, nrm,
    tok_send, tok_recv, tok_local, rs1_s, rs1_r, rs2_s, rs2_r, ag_s, ag_r, sib_s, sib_r,
):
    blocks, share, _ = q_ref.shape
    width = g_ref.shape[1]
    chips = n_ctx // 2
    half = chips * rows
    me_c, me_z = lax.axis_index("ctx"), lax.axis_index("head")
    core, chip = lax.rem(me_c, 2), me_c // 2
    sibling = me_c + 1 - 2 * core

    def mate(step):
        return lax.rem(chip + step, chips) * 2 + core

    def peer(step):
        return lax.rem(me_z + step, n_head)

    barrier = pltpu.get_barrier_semaphore()
    for step in range(1, n_head):
        pl.semaphore_signal(barrier, inc=1, device_id={"head": peer(step)}, device_id_type=MESH)
    for step in range(1, chips):
        pl.semaphore_signal(barrier, inc=1, device_id={"ctx": mate(step)}, device_id_type=MESH)
    pl.semaphore_signal(barrier, inc=1, device_id={"ctx": sibling}, device_id_type=MESH)
    pl.semaphore_wait(barrier, n_head - 1 + chips)

    def columns(head):
        return pl.ds(pl.multiple_of(head * width, TILE), width)

    def remote(src, dst, send, recv, device):
        copy = pltpu.make_async_remote_copy(
            src_ref=src, dst_ref=dst, send_sem=send, recv_sem=recv, device_id=device, device_id_type=MESH
        )
        copy.start()
        return copy

    def spread(kind, block, source, landing):
        copies = []
        for step in range(1, n_head):
            copies.append(remote(
                source.at[block, :, columns(peer(step))], landing.at[block, me_z],
                tok_send.at[kind, block, step], tok_recv.at[kind, block, step], {"head": peer(step)},
            ))
        local = pltpu.make_async_copy(
            source.at[block, :, columns(me_z)], landing.at[block, me_z], tok_local.at[kind, block]
        )
        local.start()
        return copies, local

    def sent(copies):
        for copy in copies[0]:
            copy.wait_send()

    def arrived(copies):
        for copy in copies[0]:
            copy.wait_recv()
        copies[1].wait()

    def scale_values(block):
        for head in range(n_head):
            cols = slice(head * width, (head + 1) * width)
            rate = r_ref[block, :, head:head + 1].astype(f32)
            tgt[block, :, cols] = (v_ref[block, :, cols].astype(f32) * rate).astype(bf16)

    def grads(block):
        def chunk(z, carry):
            at = pl.ds(pl.multiple_of(z * share, 16), share)
            pre = dot(kx[block, z], wb[block, :2 * width, :], NT)
            pre_gate, pre_up = pre[:, :width], pre[:, width:]
            sigma = jax.nn.sigmoid(pre_gate)
            silu = pre_gate * sigma
            hid[at, :] = silu * pre_up
            back = dot(tx[block, z], wb[block, 2 * width:3 * width, :], NN)
            dgu[at, :width] = back * pre_up * sigma * (1.0 + pre_gate * (1.0 - sigma))
            dgu[at, width:] = back * silu
            return carry

        lax.fori_loop(0, n_head, chunk, 0)
        keys = kx[block].reshape(n_head * share, width)

        def key_tile(i, carry):
            at = pl.ds(pl.multiple_of(i * TILE, TILE), TILE)
            gb[block, at, :] = dot_split(dgu[:, at], keys, TN).astype(bf16)
            return carry

        lax.fori_loop(0, 2 * width // TILE, key_tile, 0)
        targets = tx[block].reshape(n_head * share, width)

        def down_tile(i, carry):
            at = pl.ds(pl.multiple_of(i * TILE, TILE), TILE)
            to = pl.ds(pl.multiple_of(2 * width + i * TILE, TILE), TILE)
            high = hid[...].astype(bf16)
            low = (hid[...] - high.astype(f32)).astype(bf16)
            tile = tx[block, :, :, at].reshape(n_head * share, TILE)
            gb[block, to, :] = (dot(tile, high, TN) + dot(tile, low, TN)).astype(bf16)
            return carry

        lax.fori_loop(0, width // TILE, down_tile, 0)
        if n_ctx * rows > 3 * width:
            gb[block, 3 * width:, :] = jnp.zeros((n_ctx * rows - 3 * width, width), bf16)

    def shard(of_core, of_chip):
        return pl.ds(pl.multiple_of((of_core * chips + of_chip) * rows, 16), rows)

    mine = shard(core, chip)
    pending = []

    def reduce_start(block):
        first = {}
        for step in list(range(1, chips)) + [0]:
            other = lax.rem(chip + step, chips)
            first[step] = remote(
                gb.at[block, shard(1 - core, other)], rb1.at[block, step],
                rs1_s.at[block, step], rs1_r.at[block, step], {"ctx": sibling},
            )
        second = []
        for step in range(1, chips):
            other = lax.rem(chip + step, chips)
            first[step].wait_recv()
            pair = gb[block, shard(core, other), :].astype(f32) + rb1[block, step].astype(f32)
            sb[block, step] = pair.astype(bf16)
            second.append(remote(
                sb.at[block, step], rb2.at[block, step],
                rs2_s.at[block, step], rs2_r.at[block, step], {"ctx": mate(step)},
            ))
        pending.extend(first.values())
        pending.extend(second)
        return first[0], second

    def reduce_finish(block, state, norm):
        own, second = state
        own.wait_recv()
        total = gb[block, mine, :].astype(f32) + rb1[block, 0].astype(f32)
        for step, copy in enumerate(second):
            copy.wait_recv()
            total = total + rb2[block, step + 1].astype(f32)
        fresh = mst[...] + total
        fresh = fresh * (norm * lax.rsqrt(jnp.sum(fresh * fresh, axis=1, keepdims=True) + 1e-06))
        mst[...] = fresh
        wb[block + 1, mine, :] = fresh.astype(bf16)
        out = [
            remote(
                wb.at[block + 1, mine], wb.at[block + 1, mine],
                ag_s.at[block, step], ag_r.at[block, step], {"ctx": mate(step)},
            )
            for step in range(1, chips)
        ]
        pair = [remote(
            wb.at[block + 1, mine], wb.at[block + 1, mine], sib_s.at[block, 0], sib_r.at[block, 0], {"ctx": sibling}
        )]
        return out, pair

    def share_finish(block, state):
        out, pair = state
        for step, copy in enumerate(out):
            copy.wait_recv()
            origin = shard(core, lax.rem(chip + chips - step - 1, chips))
            pair.append(remote(
                wb.at[block + 1, origin], wb.at[block + 1, origin],
                sib_s.at[block, step + 1], sib_r.at[block, step + 1], {"ctx": sibling},
            ))
        for copy in pair:
            copy.wait_recv()
        pending.extend(out)
        pending.extend(pair)

    def apply(block):
        def chunk(z, carry):
            at = pl.ds(pl.multiple_of(z * share, 16), share)
            pre = dot(qx[block, z], wb[block + 1, :2 * width, :], NT)
            pre_gate = pre[:, :width]
            hidden = pre_gate * jax.nn.sigmoid(pre_gate) * pre[:, width:]
            out = dot_split(hidden, wb[block + 1, 2 * width:3 * width, :], NT)
            scale = lax.rsqrt(jnp.mean(out * out, axis=-1, keepdims=True) + 1e-05)
            nrm[block, at, :] = (out * scale * gain_ref[...]).astype(bf16)
            return carry

        lax.fori_loop(0, n_head, chunk, 0)
        copies = []
        for step in range(1, n_head):
            at = pl.ds(pl.multiple_of(peer(step) * share, 16), share)
            copies.append(remote(
                nrm.at[block, at], o_ref.at[block, :, columns(me_z)],
                tok_send.at[3, block, step], tok_recv.at[3, block, step], {"head": peer(step)},
            ))
        at = pl.ds(pl.multiple_of(me_z * share, 16), share)
        local = pltpu.make_async_copy(
            nrm.at[block, at], o_ref.at[block, :, columns(me_z)], tok_local.at[3, block]
        )
        local.start()
        return copies, local

    key_sends = [spread(0, 0, k_ref, kx)]
    scale_values(0)
    tgt_sends = [spread(1, 0, tgt, tx)]
    for block in range(1, blocks):
        scale_values(block)
    for index, ref in enumerate((g_ref, u_ref, d_ref)):
        def turn(i, carry, ref=ref, index=index):
            at = pl.ds(pl.multiple_of(i * TILE, TILE), TILE)
            to = pl.ds(pl.multiple_of(index * width + i * TILE, TILE), TILE)
            tile = ref[0, :, at].T
            wt[to, :] = tile
            wb[0, to, :] = tile.astype(bf16)
            return carry

        lax.fori_loop(0, width // TILE, turn, 0)
    if n_ctx * rows > 3 * width:
        wt[3 * width:, :] = jnp.zeros((n_ctx * rows - 3 * width, width), f32)
    mst[...] = wt[mine, :]
    norm = jnp.sqrt(jnp.sum(mst[...] * mst[...], axis=1, keepdims=True))

    query_sends, results = [], []
    for block in range(blocks):
        ahead = block + 1 < blocks
        if ahead:
            sent(key_sends[block])
            key_sends.append(spread(0, block + 1, k_ref, kx))
        arrived(key_sends[block])
        if ahead:
            sent(tgt_sends[block])
            tgt_sends.append(spread(1, block + 1, tgt, tx))
        arrived(tgt_sends[block])
        grads(block)
        state = reduce_start(block)
        if block > 0:
            arrived(query_sends[block - 1])
            results.append(apply(block - 1))
        state = reduce_finish(block, state, norm)
        query_sends.append(spread(2, block, q_ref, qx))
        share_finish(block, state)
    sent(key_sends[-1])
    sent(tgt_sends[-1])
    arrived(query_sends[-1])
    results.append(apply(blocks - 1))
    for copies in query_sends:
        sent(copies)
    for copies in results:
        arrived(copies)
        sent(copies)
    for copy in pending:
        copy.wait_send()


def gather_proj(out_proj):
    cols = out_proj.shape[1] // lax.axis_size("ctx")
    piece = lax.dynamic_slice_in_dim(out_proj, lax.axis_index("ctx") * cols, cols, 1)
    piece = lax.all_gather(piece, "head", axis=0, tiled=True)
    return lax.all_gather(piece, "ctx", axis=1, tiled=True)


def per_device(queries, keys, values, rates, gate_fast, up_fast, down_fast, out_gain, out_proj):
    blocks, share, _ = queries.shape
    width = gate_fast.shape[1]
    n_ctx, n_head = lax.axis_size("ctx"), lax.axis_size("head")
    chips = n_ctx // 2
    rows = -(-3 * width // (16 * n_ctx)) * 16
    dma = pltpu.SemaphoreType.DMA
    landing = pltpu.VMEM((blocks, n_head, share, width), bf16)
    exchange = pltpu.VMEM((blocks, chips, rows, width), bf16)
    vmem = pl.BlockSpec(memory_space=pltpu.VMEM)
    anywhere = pl.BlockSpec(memory_space=pl.ANY)
    proj = gather_proj(out_proj)
    normed = pl.pallas_call(
        functools.partial(kernel, n_ctx, n_head, rows),
        out_shape=jax.ShapeDtypeStruct(queries.shape, bf16),
        in_specs=[anywhere] * 2 + [vmem] * 6,
        out_specs=vmem,
        scratch_shapes=[
            pltpu.VMEM(values.shape, bf16),
            landing, landing, landing,
            pltpu.VMEM((blocks + 1, n_ctx * rows, width), bf16),
            pltpu.VMEM((n_ctx * rows, width), f32),
            pltpu.VMEM((rows, width), f32),
            pltpu.VMEM((blocks, n_ctx * rows, width), bf16),
            exchange, exchange, exchange,
            pltpu.VMEM((n_head * share, 2 * width), f32),
            pltpu.VMEM((n_head * share, width), f32),
            pltpu.VMEM((blocks, n_head * share, width), bf16),
            dma((4, blocks, n_head)), dma((4, blocks, n_head)), dma((4, blocks)),
        ] + [dma((blocks, chips))] * 8,
        compiler_params=pltpu.CompilerParams(
            collective_id=0, has_side_effects=True, vmem_limit_bytes=60 * 1024 * 1024
        ),
        cost_estimate=pl.CostEstimate(flops=20_000_000_000, bytes_accessed=300_000_000, transcendentals=0),
    )(queries, keys, values, rates, gate_fast, up_fast, down_fast, out_gain[None, :])
    return jnp.einsum("btf,fd->btd", normed, proj, preferred_element_type=f32).astype(bf16)


def solution(mesh):
    tokens = P(None, ("ctx", "head"), None)
    matrix = P("head", None, None)
    return jax.shard_map(
        per_device,
        mesh=mesh,
        in_specs=(tokens,) * 4 + (matrix,) * 3 + (P("head"), P("head", None)),
        out_specs=tokens,
        check_vma=False,
    )
```

```python
import functools

import jax
import jax.numpy as jnp
from jax import lax
from jax.experimental import pallas as pl
from jax.experimental.pallas import tpu as pltpu
from jax.sharding import PartitionSpec as P

bf16 = jnp.bfloat16
f32 = jnp.float32
MESH = pl.DeviceIdType.MESH
NN = (((1,), (0,)), ((), ()))
NT = (((1,), (1,)), ((), ()))
TN = (((0,), (0,)), ((), ()))
TILE = 128


def dot(left, right, dims):
    return lax.dot_general(left, right, dims, preferred_element_type=f32)


def dot_split(left, right, dims):
    high = left.astype(bf16)
    low = (left - high.astype(f32)).astype(bf16)
    return dot(high, right, dims) + dot(low, right, dims)


def kernel(
    n_ctx, n_head, rows,
    q_ref, k_ref, v_ref, r_ref, kx0, tx0, w0, m0, gain_ref,
    o_ref,
    tgt, kx, tx, qx, wb, mst, gb, rb1, sb, rb2, dgu, hid, nrm,
    tok_send, tok_recv, tok_local, rs1_s, rs1_r, rs2_s, rs2_r, ag_s, ag_r, sib_s, sib_r,
):
    blocks, share, _ = q_ref.shape
    width = w0.shape[1]
    chips = n_ctx // 2
    half = chips * rows
    me_c, me_z = lax.axis_index("ctx"), lax.axis_index("head")
    core, chip = lax.rem(me_c, 2), me_c // 2
    sibling = me_c + 1 - 2 * core

    def mate(step):
        return lax.rem(chip + step, chips) * 2 + core

    def peer(step):
        return lax.rem(me_z + step, n_head)

    barrier = pltpu.get_barrier_semaphore()
    for step in range(1, n_head):
        pl.semaphore_signal(barrier, inc=1, device_id={"head": peer(step)}, device_id_type=MESH)
    for step in range(1, chips):
        pl.semaphore_signal(barrier, inc=1, device_id={"ctx": mate(step)}, device_id_type=MESH)
    pl.semaphore_signal(barrier, inc=1, device_id={"ctx": sibling}, device_id_type=MESH)
    pl.semaphore_wait(barrier, n_head - 1 + chips)

    def columns(head):
        return pl.ds(pl.multiple_of(head * width, TILE), width)

    def remote(src, dst, send, recv, device):
        copy = pltpu.make_async_remote_copy(
            src_ref=src, dst_ref=dst, send_sem=send, recv_sem=recv, device_id=device, device_id_type=MESH
        )
        copy.start()
        return copy

    def spread(kind, block, source, landing):
        copies = []
        for step in range(1, n_head):
            copies.append(remote(
                source.at[block, :, columns(peer(step))], landing.at[block, me_z],
                tok_send.at[kind, block, step], tok_recv.at[kind, block, step], {"head": peer(step)},
            ))
        local = pltpu.make_async_copy(
            source.at[block, :, columns(me_z)], landing.at[block, me_z], tok_local.at[kind, block]
        )
        local.start()
        return copies, local

    def sent(copies):
        for copy in copies[0]:
            copy.wait_send()

    def arrived(copies):
        for copy in copies[0]:
            copy.wait_recv()
        copies[1].wait()

    def scale_values(block):
        for head in range(n_head):
            cols = slice(head * width, (head + 1) * width)
            rate = r_ref[block, :, head:head + 1].astype(f32)
            tgt[block, :, cols] = (v_ref[block, :, cols].astype(f32) * rate).astype(bf16)

    def grads(block):
        kin = kx.at[block] if block else kx0
        tin = tx.at[block] if block else tx0
        win = wb.at[block] if block else w0

        def chunk(z, carry):
            at = pl.ds(pl.multiple_of(z * share, 16), share)
            pre = dot(kin[z], win[:2 * width, :], NT)
            pre_gate, pre_up = pre[:, :width], pre[:, width:]
            sigma = jax.nn.sigmoid(pre_gate)
            silu = pre_gate * sigma
            hid[at, :] = silu * pre_up
            back = dot(tin[z], win[2 * width:3 * width, :], NN)
            dgu[at, :width] = back * pre_up * sigma * (1.0 + pre_gate * (1.0 - sigma))
            dgu[at, width:] = back * silu
            return carry

        lax.fori_loop(0, n_head, chunk, 0)
        keys = kin[...].reshape(n_head * share, width)

        def key_tile(i, carry):
            at = pl.ds(pl.multiple_of(i * TILE, TILE), TILE)
            gb[block, at, :] = dot_split(dgu[:, at], keys, TN).astype(bf16)
            return carry

        lax.fori_loop(0, 2 * width // TILE, key_tile, 0)

        def down_tile(i, carry):
            at = pl.ds(pl.multiple_of(i * TILE, TILE), TILE)
            to = pl.ds(pl.multiple_of(2 * width + i * TILE, TILE), TILE)
            high = hid[...].astype(bf16)
            low = (hid[...] - high.astype(f32)).astype(bf16)
            tile = tin[:, :, at].reshape(n_head * share, TILE)
            gb[block, to, :] = (dot(tile, high, TN) + dot(tile, low, TN)).astype(bf16)
            return carry

        lax.fori_loop(0, width // TILE, down_tile, 0)
        if n_ctx * rows > 3 * width:
            gb[block, 3 * width:, :] = jnp.zeros((n_ctx * rows - 3 * width, width), bf16)

    def shard(of_core, of_chip):
        return pl.ds(pl.multiple_of((of_core * chips + of_chip) * rows, 16), rows)

    mine = shard(core, chip)
    pending = []

    def reduce_start(block):
        first = {}
        for step in list(range(1, chips)) + [0]:
            other = lax.rem(chip + step, chips)
            first[step] = remote(
                gb.at[block, shard(1 - core, other)], rb1.at[block, step],
                rs1_s.at[block, step], rs1_r.at[block, step], {"ctx": sibling},
            )
        second = []
        for step in range(1, chips):
            other = lax.rem(chip + step, chips)
            first[step].wait_recv()
            pair = gb[block, shard(core, other), :].astype(f32) + rb1[block, step].astype(f32)
            sb[block, step] = pair.astype(bf16)
            second.append(remote(
                sb.at[block, step], rb2.at[block, step],
                rs2_s.at[block, step], rs2_r.at[block, step], {"ctx": mate(step)},
            ))
        pending.extend(first.values())
        pending.extend(second)
        return first[0], second

    def reduce_finish(block, state, norm):
        own, second = state
        own.wait_recv()
        total = gb[block, mine, :].astype(f32) + rb1[block, 0].astype(f32)
        for step, copy in enumerate(second):
            copy.wait_recv()
            total = total + rb2[block, step + 1].astype(f32)
        fresh = mst[...] + total
        fresh = fresh * (norm * lax.rsqrt(jnp.sum(fresh * fresh, axis=1, keepdims=True) + 1e-06))
        mst[...] = fresh
        wb[block + 1, mine, :] = fresh.astype(bf16)
        out = [
            remote(
                wb.at[block + 1, mine], wb.at[block + 1, mine],
                ag_s.at[block, step], ag_r.at[block, step], {"ctx": mate(step)},
            )
            for step in range(1, chips)
        ]
        pair = [remote(
            wb.at[block + 1, mine], wb.at[block + 1, mine], sib_s.at[block, 0], sib_r.at[block, 0], {"ctx": sibling}
        )]
        return out, pair

    def share_finish(block, state):
        out, pair = state
        for step, copy in enumerate(out):
            copy.wait_recv()
            origin = shard(core, lax.rem(chip + chips - step - 1, chips))
            pair.append(remote(
                wb.at[block + 1, origin], wb.at[block + 1, origin],
                sib_s.at[block, step + 1], sib_r.at[block, step + 1], {"ctx": sibling},
            ))
        for copy in pair:
            copy.wait_recv()
        pending.extend(out)
        pending.extend(pair)

    def apply(block):
        def chunk(z, carry):
            at = pl.ds(pl.multiple_of(z * share, 16), share)
            pre = dot(qx[block, z], wb[block + 1, :2 * width, :], NT)
            pre_gate = pre[:, :width]
            hidden = pre_gate * jax.nn.sigmoid(pre_gate) * pre[:, width:]
            out = dot_split(hidden, wb[block + 1, 2 * width:3 * width, :], NT)
            scale = lax.rsqrt(jnp.mean(out * out, axis=-1, keepdims=True) + 1e-05)
            nrm[block, at, :] = (out * scale * gain_ref[...]).astype(bf16)
            return carry

        lax.fori_loop(0, n_head, chunk, 0)
        copies = []
        for step in range(1, n_head):
            at = pl.ds(pl.multiple_of(peer(step) * share, 16), share)
            copies.append(remote(
                nrm.at[block, at], o_ref.at[block, :, columns(me_z)],
                tok_send.at[3, block, step], tok_recv.at[3, block, step], {"head": peer(step)},
            ))
        at = pl.ds(pl.multiple_of(me_z * share, 16), share)
        local = pltpu.make_async_copy(
            nrm.at[block, at], o_ref.at[block, :, columns(me_z)], tok_local.at[3, block]
        )
        local.start()
        return copies, local

    key_sends, tgt_sends = [None], [None]
    if blocks > 1:
        key_sends.append(spread(0, 1, k_ref, kx))
        scale_values(1)
        tgt_sends.append(spread(1, 1, tgt, tx))
    for block in range(2, blocks):
        scale_values(block)
    mst[...] = m0[...]
    norm = jnp.sqrt(jnp.sum(mst[...] * mst[...], axis=1, keepdims=True))

    query_sends, results = [], []
    for block in range(blocks):
        if block > 0:
            ahead = block + 1 < blocks
            sent(key_sends[block])
            if ahead:
                key_sends.append(spread(0, block + 1, k_ref, kx))
            arrived(key_sends[block])
            sent(tgt_sends[block])
            if ahead:
                tgt_sends.append(spread(1, block + 1, tgt, tx))
            arrived(tgt_sends[block])
        grads(block)
        state = reduce_start(block)
        if block > 0:
            arrived(query_sends[block - 1])
            results.append(apply(block - 1))
        state = reduce_finish(block, state, norm)
        query_sends.append(spread(2, block, q_ref, qx))
        share_finish(block, state)
    arrived(query_sends[-1])
    results.append(apply(blocks - 1))
    for copies in query_sends:
        sent(copies)
    for copies in results:
        arrived(copies)
        sent(copies)
    for copy in pending:
        copy.wait_send()


def opening(
    n_ctx, n_head, rows,
    k_ref, v_ref, r_ref, g_ref, u_ref, d_ref,
    kx0, tx0, w0, m0,
    tgt, wt, send, recv, here,
):
    share = k_ref.shape[1]
    width = g_ref.shape[1]
    chips = n_ctx // 2
    me_c, me_z = lax.axis_index("ctx"), lax.axis_index("head")

    def peer(step):
        return lax.rem(me_z + step, n_head)

    def columns(head):
        return pl.ds(pl.multiple_of(head * width, TILE), width)

    barrier = pltpu.get_barrier_semaphore()
    for step in range(1, n_head):
        pl.semaphore_signal(barrier, inc=1, device_id={"head": peer(step)}, device_id_type=MESH)
    pl.semaphore_wait(barrier, n_head - 1)
    copies = []

    def spread(kind, source, landing):
        for step in range(1, n_head):
            copies.append(pltpu.make_async_remote_copy(
                src_ref=source.at[:, columns(peer(step))], dst_ref=landing.at[me_z],
                send_sem=send.at[kind, step], recv_sem=recv.at[kind, step],
                device_id={"head": peer(step)}, device_id_type=MESH,
            ))
            copies[-1].start()
        copies.append(pltpu.make_async_copy(source.at[:, columns(me_z)], landing.at[me_z], here.at[kind]))
        copies[-1].start()

    spread(0, k_ref.at[0], kx0)
    for head in range(n_head):
        cols = slice(head * width, (head + 1) * width)
        rate = r_ref[0, :, head:head + 1].astype(f32)
        tgt[:, cols] = (v_ref[0, :, cols].astype(f32) * rate).astype(bf16)
    spread(1, tgt, tx0)
    for index, ref in enumerate((g_ref, u_ref, d_ref)):
        def turn(i, carry, ref=ref, index=index):
            at = pl.ds(pl.multiple_of(i * TILE, TILE), TILE)
            to = pl.ds(pl.multiple_of(index * width + i * TILE, TILE), TILE)
            tile = ref[0, :, at].T
            wt[to, :] = tile
            w0[to, :] = tile.astype(bf16)
            return carry

        lax.fori_loop(0, width // TILE, turn, 0)
    if n_ctx * rows > 3 * width:
        wt[3 * width:, :] = jnp.zeros((n_ctx * rows - 3 * width, width), f32)
        w0[3 * width:, :] = jnp.zeros((n_ctx * rows - 3 * width, width), bf16)
    own = lax.rem(me_c, 2) * chips + me_c // 2
    m0[...] = wt[pl.ds(pl.multiple_of(own * rows, 16), rows), :]
    for copy in copies:
        copy.wait()


def per_device(queries, keys, values, rates, gate_fast, up_fast, down_fast, out_gain, out_proj):
    blocks, share, _ = queries.shape
    width = gate_fast.shape[1]
    n_ctx, n_head = lax.axis_size("ctx"), lax.axis_size("head")
    chips = n_ctx // 2
    rows = -(-3 * width // (16 * n_ctx)) * 16
    dma = pltpu.SemaphoreType.DMA
    landing = pltpu.VMEM((blocks, n_head, share, width), bf16)
    exchange = pltpu.VMEM((blocks, chips, rows, width), bf16)
    vmem = pl.BlockSpec(memory_space=pltpu.VMEM)
    anywhere = pl.BlockSpec(memory_space=pl.ANY)
    cols = out_proj.shape[1] // n_ctx
    piece = lax.dynamic_slice_in_dim(out_proj, lax.axis_index("ctx") * cols, cols, 1)
    piece = lax.all_gather(piece, "head", axis=0, tiled=True)
    arrivals = jax.ShapeDtypeStruct((n_head, share, width), bf16)
    opened = pl.pallas_call(
        functools.partial(opening, n_ctx, n_head, rows),
        out_shape=[
            arrivals, arrivals,
            jax.ShapeDtypeStruct((n_ctx * rows, width), bf16),
            jax.ShapeDtypeStruct((rows, width), f32),
        ],
        in_specs=[anywhere] + [vmem] * 5,
        out_specs=[vmem] * 4,
        scratch_shapes=[
            pltpu.VMEM(values.shape[1:], bf16),
            pltpu.VMEM((n_ctx * rows, width), f32),
            dma((2, n_head)), dma((2, n_head)), dma((2,)),
        ],
        compiler_params=pltpu.CompilerParams(
            collective_id=1, has_side_effects=True, vmem_limit_bytes=40 * 1024 * 1024
        ),
        cost_estimate=pl.CostEstimate(flops=0, bytes_accessed=120_000_000, transcendentals=0),
    )(keys, values, rates, gate_fast, up_fast, down_fast)
    opened, piece = lax.optimization_barrier((opened, piece))
    proj = lax.all_gather(piece, "ctx", axis=1, tiled=True)
    normed = pl.pallas_call(
        functools.partial(kernel, n_ctx, n_head, rows),
        out_shape=jax.ShapeDtypeStruct(queries.shape, bf16),
        in_specs=[anywhere] * 2 + [vmem] * 7,
        out_specs=vmem,
        scratch_shapes=[
            pltpu.VMEM(values.shape, bf16),
            landing, landing, landing,
            pltpu.VMEM((blocks + 1, n_ctx * rows, width), bf16),
            pltpu.VMEM((rows, width), f32),
            pltpu.VMEM((blocks, n_ctx * rows, width), bf16),
            exchange, exchange, exchange,
            pltpu.VMEM((n_head * share, 2 * width), f32),
            pltpu.VMEM((n_head * share, width), f32),
            pltpu.VMEM((blocks, n_head * share, width), bf16),
            dma((4, blocks, n_head)), dma((4, blocks, n_head)), dma((4, blocks)),
        ] + [dma((blocks, chips))] * 8,
        compiler_params=pltpu.CompilerParams(
            collective_id=0, has_side_effects=True, vmem_limit_bytes=60 * 1024 * 1024
        ),
        cost_estimate=pl.CostEstimate(flops=20_000_000_000, bytes_accessed=300_000_000, transcendentals=0),
    )(queries, keys, values, rates, *opened, out_gain[None, :])
    return jnp.einsum("btf,fd->btd", normed, proj, preferred_element_type=f32).astype(bf16)


def solution(mesh):
    tokens = P(None, ("ctx", "head"), None)
    matrix = P("head", None, None)
    return jax.shard_map(
        per_device,
        mesh=mesh,
        in_specs=(tokens,) * 4 + (matrix,) * 3 + (P("head"), P("head", None)),
        out_specs=tokens,
        check_vma=False,
    )
```
